32 devices in a mesh: group: 8 (over z, x), module: 4 (over y, core).
Axes of the slice: x: 2, y: 2, z: 4, core: 2. Of those that a mesh axis runs over, the one named last changes fastest.
Arguments:
- train_grads: bfloat16 [2048, 4, 1024], P(('group', 'module')), may hold values from -6 to 6
- query_grads: bfloat16 [8, 32, 4, 1024], P('group', None, 'module'), may hold values from -6 to 6
- basis_out: bfloat16 [4, 32, 32], P('module'), may hold values from -1 to 1
- basis_in: bfloat16 [4, 32, 32], P('module'), may hold values from -1 to 1
- eigenvalues: float32 [4, 1024], P('module'), may hold values from 0.05 to 5
- owner_groups: int32 [4], replicated, may hold values from 0 to 7, as said below
- module_order: int32 [4], replicated, may hold values from 0 to 3, each once
Outputs:
- scores: float32 [2048, 128], P(('group', 'module'))
The draws below stay inside these ranges and needn't reach their ends.
Inputs may be any that keep to these rules, and one draw needn't show every extreme that they name: `owner_groups`: 4 different groups, the first and the last group among them. `module_order`: each module exactly once.
All inputs are finite; a program needn't handle non-finite values.
Results may differ from the reference program's by a relative error of at most 0.0037.
Values may be sent and summed in bfloat16 or wider, within the bound.
No kernel may reach another device: no remote copies, remote signals or barrier semaphores. Data moves between devices by JAX's collectives and lax.ppermute only.
A program may use at most 64 MiB of HBM per device.

```python
import math
import jax
import jax.numpy as jnp
from jax import lax

SIDE = 32
W = 1024
MODULES = 4
EXAMPLES = 2048
QPO = 32
OWNERS = 4
QUERIES = 128
N_GROUP = 8


def draw_owner_groups(key, part):
    middle = jax.random.permutation(jax.random.fold_in(key, 11), N_GROUP - 2)[:OWNERS - 2] + 1
    joined = jnp.concatenate([jnp.zeros((1,), jnp.int32), middle.astype(jnp.int32), jnp.full((1,), N_GROUP - 1, jnp.int32)])
    shuffle = jax.random.permutation(jax.random.fold_in(key, 12), OWNERS)
    return joined[shuffle].astype(jnp.int32)


def level_of(own_key, extent, cuts, least, high):
    def one(axis_at, blocks):
        draws = jax.random.uniform(jax.random.fold_in(jax.random.fold_in(own_key, 6), axis_at), (blocks,), jnp.float32, least / len(cuts), high / len(cuts))
        return jnp.repeat(jnp.exp(draws), extent[axis_at] // blocks).reshape((-1,) + (1,) * (len(extent) - axis_at - 1))

    loudness = one(*cuts[0])
    for cut in cuts[1:]:
        loudness = loudness * one(*cut)
    return loudness


def centred(rng, shape, width, most, shards=(), kind=jnp.bfloat16):
    entries = width * jax.random.normal(rng, shape, jnp.float32)
    if shards:
        entries = entries * level_of(rng, shape, shards, -0.22, 0.18)
    return jnp.clip(entries, -most, most).astype(kind)


def setup_inputs(seed: int = 0) -> dict:
    streams_of = jax.random.split(jax.random.key(seed), 8)
    return {
        "train_grads": centred(streams_of[0], (EXAMPLES, MODULES, W), 1.0, 6.0, ((0, 32),)),
        "query_grads": centred(streams_of[1], (N_GROUP, QPO, MODULES, W), 1.0, 6.0, ((0, 8), (2, 4))),
        "basis_out": centred(streams_of[2], (MODULES, SIDE, SIDE), SIDE ** -0.5, 1.0, ((0, 4),)),
        "basis_in": centred(streams_of[3], (MODULES, SIDE, SIDE), SIDE ** -0.5, 1.0, ((0, 4),)),
        "eigenvalues": jnp.clip(jnp.exp(math.log(5.0) - 4.6051702 * jax.random.uniform(streams_of[4], (MODULES, W), jnp.float32) ** level_of(streams_of[4], (MODULES, W), ((0, 4),), -0.2, 0.2)), 0.05, 5.0),
        "owner_groups": draw_owner_groups(jax.random.fold_in(streams_of[7], 71), 0),
        "module_order": jax.random.permutation(streams_of[6], MODULES).astype(jnp.int32),
    }


def build_rotator(basis_out, basis_in):
    breadth = basis_out.shape[-1]
    product = basis_out.astype(jnp.float32)[..., :, None, :, None] * basis_in.astype(jnp.float32)[..., None, :, None, :]
    return product.reshape(basis_out.shape[:-2] + (breadth * breadth, breadth * breadth)).astype(jnp.bfloat16)

def reference(train_grads, query_grads, basis_out, basis_in, eigenvalues, owner_groups, module_order):
    queries = jnp.take(query_grads, owner_groups, axis=0).reshape(QUERIES, MODULES, W)

    def add_slot(running, slot_index):
        rotator = build_rotator(basis_out[slot_index], basis_in[slot_index])
        spectrum = eigenvalues[slot_index]
        damping = 0.1 * jnp.mean(spectrum)
        column = lax.dynamic_index_in_dim(train_grads, module_order[slot_index], axis=1, keepdims=False)
        turned = jnp.dot(column, rotator, preferred_element_type=jnp.float32).astype(jnp.bfloat16)
        asked = (jnp.dot(queries[:, slot_index], rotator, preferred_element_type=jnp.float32) / (spectrum + damping)).astype(jnp.bfloat16)
        return (running + jnp.dot(turned, asked.T, preferred_element_type=jnp.float32), None)
    running = jnp.zeros((EXAMPLES, QUERIES), jnp.float32)
    running, unused = lax.scan(add_slot, running, jnp.arange(MODULES, dtype=jnp.int32))
    return running / math.sqrt(MODULES * W)
```

```python
import functools
import math

import jax
import jax.numpy as jnp
from jax import lax
from jax.experimental import pallas as pl
from jax.experimental.pallas import tpu as pltpu
from jax.sharding import PartitionSpec as P

VMEM = pl.BlockSpec(memory_space=pltpu.VMEM)
SMEM = pl.BlockSpec(memory_space=pltpu.SMEM)
LANES = 128
PARAMS = pltpu.CompilerParams(vmem_limit_bytes=32 * 1024 * 1024)


def slots_kernel(order_ref, train_ref, *refs):
    outs, wide = refs[:-1], refs[-1]
    rows, modules, _ = train_ref.shape
    me = lax.axis_index("module")
    tiles = wide.shape[0] // (rows * modules)
    for e in range(rows):
        example = train_ref[e].astype(jnp.float32)
        for t in range(tiles):
            wide[pl.ds((t * rows + e) * modules, modules), :] = example[:, t * LANES : (t + 1) * LANES]
    for j, out in enumerate(outs):
        held = order_ref[me ^ j]
        for t in range(tiles):
            piece = wide[pl.ds(t * rows * modules + held, rows, stride=modules), :]
            out[:, t * LANES : (t + 1) * LANES] = piece.astype(out.dtype)


def by_slot(module_order, train_grads):
    rows, modules, width = train_grads.shape
    piece = jax.ShapeDtypeStruct((rows, width), train_grads.dtype)
    return pl.pallas_call(
        slots_kernel,
        out_shape=(piece,) * modules,
        in_specs=[SMEM, VMEM],
        out_specs=(VMEM,) * modules,
        scratch_shapes=[pltpu.VMEM((rows * modules * width // LANES, LANES), jnp.float32)],
        compiler_params=PARAMS,
    )(module_order, train_grads)


def rotator_kernel(out_ref, in_ref, rotator_ref):
    side = out_ref.shape[0]
    width = rotator_ref.shape[0]
    column = lax.broadcasted_iota(jnp.int32, (side, width), 1)
    row = lax.broadcasted_iota(jnp.int32, (side, width), 0)
    spread = (column // side == row).astype(jnp.bfloat16)
    tiled = (column % side == row).astype(jnp.bfloat16)
    outer = jnp.dot(out_ref[...], spread, preferred_element_type=jnp.float32)
    inner = jnp.dot(in_ref[...], tiled, preferred_element_type=jnp.float32)
    for a in range(side):
        rotator_ref[pl.ds(a * side, side), :] = (outer[a : a + 1, :] * inner).astype(jnp.bfloat16)


def rotator_of(basis_out, basis_in):
    width = basis_out.shape[0] ** 2
    return pl.pallas_call(
        rotator_kernel,
        out_shape=jax.ShapeDtypeStruct((width, width), jnp.bfloat16),
        in_specs=[VMEM, VMEM],
        out_specs=VMEM,
        compiler_params=PARAMS,
    )(basis_out, basis_in)


def turn_kernel(rotator_ref, *refs):
    count = len(refs) // 2
    for piece, turned in zip(refs[:count], refs[count:]):
        turned[...] = jnp.dot(
            piece[...], rotator_ref[...], preferred_element_type=jnp.float32
        ).astype(turned.dtype)


def turn(rotator, pieces):
    return pl.pallas_call(
        turn_kernel,
        out_shape=tuple(jax.ShapeDtypeStruct(p.shape, p.dtype) for p in pieces),
        in_specs=[VMEM] * (1 + len(pieces)),
        out_specs=(VMEM,) * len(pieces),
        compiler_params=PARAMS,
    )(rotator, *pieces)


def score_kernel(groups, factor, owners_ref, rotator_ref, values_ref, *refs):
    blocks, refs = refs[:groups], refs[groups:]
    queries, refs = refs[-1], refs[:-1]
    count = len(refs) // 2
    turned, outs = refs[:count], refs[count:]
    each = blocks[0].shape[0]
    me = lax.axis_index("group")
    for k in range(owners_ref.shape[0]):
        wanted = owners_ref[k] ^ me
        for b, block in enumerate(blocks):

            @pl.when(wanted == b)
            def _():
                queries[pl.ds(k * each, each), :] = block[...]

    values = values_ref[...]
    divisor = values + 0.1 * jnp.mean(values, axis=1, keepdims=True)
    asked = (
        jnp.dot(queries[...], rotator_ref[...], preferred_element_type=jnp.float32) / divisor
    ).astype(jnp.bfloat16)
    for piece, out in zip(turned, outs):
        out[...] = factor * lax.dot_general(
            piece[...], asked, (((1,), (1,)), ((), ())), preferred_element_type=jnp.float32
        )


def scores_of(owner_groups, rotator, eigenvalues, blocks, turned, factor):
    each, width = blocks[0].shape
    asked_rows = owner_groups.shape[0] * each
    return pl.pallas_call(
        functools.partial(score_kernel, len(blocks), factor),
        out_shape=tuple(
            jax.ShapeDtypeStruct((t.shape[0], asked_rows), jnp.float32) for t in turned
        ),
        in_specs=[SMEM] + [VMEM] * (2 + len(blocks) + len(turned)),
        out_specs=(VMEM,) * len(turned),
        scratch_shapes=[pltpu.VMEM((asked_rows, width), jnp.bfloat16)],
        compiler_params=PARAMS,
    )(owner_groups, rotator, eigenvalues, *blocks, *turned)


def swap(array, axis, bits):
    return lax.ppermute(array, axis, [(i, i ^ bits) for i in range(lax.axis_size(axis))])


def local(train_grads, query_grads, basis_out, basis_in, eigenvalues, owner_groups, module_order):
    _, modules, width = train_grads.shape
    groups = lax.axis_size("group")
    inner = 1 << ((groups.bit_length() - 1) // 2)
    own = query_grads.reshape(-1, width)
    blocks = [None] * groups
    for far in reversed(range(0, groups, inner)):
        blocks[far] = swap(own, "group", far) if far else own
    pieces = by_slot(module_order, train_grads)
    rotator = rotator_of(basis_out[0], basis_in[0])
    here = [pieces[0]] + [swap(pieces[j], "module", j) for j in range(1, modules)]
    turned = turn(rotator, here)
    for far in reversed(range(0, groups, inner)):
        for near in range(1, inner):
            blocks[far + near] = swap(blocks[far], "group", near)
    parts = scores_of(
        owner_groups, rotator, eigenvalues, blocks, turned, 1.0 / math.sqrt(modules * width)
    )
    total = parts[0]
    for j in range(1, modules):
        total = total + swap(parts[j], "module", j)
    return total


def solution(mesh):
    in_specs = (
        P(("group", "module"), None, None),
        P("group", None, "module", None),
        P("module", None, None),
        P("module", None, None),
        P("module", None),
        P(),
        P(),
    )
    out_specs = P(("group", "module"), None)
    return jax.shard_map(local, mesh=mesh, in_specs=in_specs, out_specs=out_specs, check_vma=False)
```

```python
import functools
import math

import jax
import jax.numpy as jnp
from jax import lax
from jax.experimental import pallas as pl
from jax.experimental.pallas import tpu as pltpu
from jax.sharding import PartitionSpec as P

VMEM = pl.BlockSpec(memory_space=pltpu.VMEM)
ANY = pl.BlockSpec(memory_space=pl.ANY)
SMEM = pl.BlockSpec(memory_space=pltpu.SMEM)
LANES = 128
def cost(us):
    return pl.CostEstimate(flops=0, bytes_accessed=int(us * 3.0e6), transcendentals=0)


PARAMS = pltpu.CompilerParams(vmem_limit_bytes=32 * 1024 * 1024)


def slots_kernel(order_hbm, train_hbm, *refs):
    outs, (order, train, wide, sems) = refs[:-4], refs[-4:]
    rows, modules, _ = train.shape
    tiles = wide.shape[0] // (rows * modules)
    loads = [
        pltpu.make_async_copy(order_hbm, order, sems.at[0]),
        pltpu.make_async_copy(train_hbm, train, sems.at[1]),
    ]
    for load in loads:
        load.start()
    for load in loads:
        load.wait()
    me = lax.axis_index("module")
    for e in range(rows):
        example = train[e].astype(jnp.float32)
        for t in range(tiles):
            wide[pl.ds((t * rows + e) * modules, modules), :] = example[:, t * LANES : (t + 1) * LANES]
    for j in range(modules):
        held = order[me ^ j]
        out, at = outs[j // 2], j % 2 * rows
        for t in range(tiles):
            piece = wide[pl.ds(t * rows * modules + held, rows, stride=modules), :]
            out[at : at + rows, t * LANES : (t + 1) * LANES] = piece.astype(out.dtype)


def by_slot(module_order, train_grads):
    rows, modules, width = train_grads.shape
    pair = jax.ShapeDtypeStruct((2 * rows, width), train_grads.dtype)
    shapes = (pair,) * (modules // 2)
    return pl.pallas_call(
        slots_kernel,
        out_shape=shapes,
        in_specs=[ANY, ANY],
        out_specs=(VMEM,) * len(shapes),
        scratch_shapes=[
            pltpu.SMEM(module_order.shape, jnp.int32),
            pltpu.VMEM(train_grads.shape, train_grads.dtype),
            pltpu.VMEM((rows * modules * width // LANES, LANES), jnp.float32),
            pltpu.SemaphoreType.DMA((2,)),
        ],
        compiler_params=PARAMS,
        cost_estimate=cost(0.8),
    )(module_order, train_grads)


def rotator_kernel(out_hbm, in_hbm, rotator_ref, out_ref, in_ref, sems):
    side = out_ref.shape[0]
    width = rotator_ref.shape[0]
    loads = [
        pltpu.make_async_copy(out_hbm, out_ref, sems.at[0]),
        pltpu.make_async_copy(in_hbm, in_ref, sems.at[1]),
    ]
    for load in loads:
        load.start()
    column = lax.broadcasted_iota(jnp.int32, (side, width), 1)
    row = lax.broadcasted_iota(jnp.int32, (side, width), 0)
    spread = (column // side == row).astype(jnp.bfloat16)
    tiled = (column % side == row).astype(jnp.bfloat16)
    for load in loads:
        load.wait()
    outer = jnp.dot(out_ref[...], spread, preferred_element_type=jnp.float32)
    inner = jnp.dot(in_ref[...], tiled, preferred_element_type=jnp.float32)
    for a in range(side):
        rotator_ref[pl.ds(a * side, side), :] = (outer[a : a + 1, :] * inner).astype(jnp.bfloat16)


def rotator_of(basis_out, basis_in):
    width = basis_out.shape[0] ** 2
    return pl.pallas_call(
        rotator_kernel,
        out_shape=jax.ShapeDtypeStruct((width, width), jnp.bfloat16),
        in_specs=[ANY, ANY],
        out_specs=VMEM,
        scratch_shapes=[
            pltpu.VMEM(basis_out.shape, basis_out.dtype),
            pltpu.VMEM(basis_in.shape, basis_in.dtype),
            pltpu.SemaphoreType.DMA((2,)),
        ],
        compiler_params=PARAMS,
        cost_estimate=cost(0.5),
    )(basis_out, basis_in)


def precondition_kernel(groups, owners_ref, rotator_ref, values_ref, *refs):
    blocks, (out, queries) = refs[:groups], refs[groups:]
    each = blocks[0].shape[0]
    me = lax.axis_index("group")
    for k in range(owners_ref.shape[0]):
        wanted = owners_ref[k] ^ me
        for b, block in enumerate(blocks):

            @pl.when(wanted == b)
            def _():
                queries[pl.ds(k * each, each), :] = block[...]

    values = values_ref[...]
    divisor = values + 0.1 * jnp.mean(values, axis=1, keepdims=True)
    asked = jnp.dot(queries[...], rotator_ref[...], preferred_element_type=jnp.float32) / divisor
    out[...] = lax.dot_general(
        asked.astype(jnp.bfloat16),
        rotator_ref[...],
        (((1,), (1,)), ((), ())),
        preferred_element_type=jnp.float32,
    ).astype(out.dtype)


def precondition(owner_groups, rotator, eigenvalues, blocks):
    each, width = blocks[0].shape
    rows = owner_groups.shape[0] * each
    return pl.pallas_call(
        functools.partial(precondition_kernel, len(blocks)),
        out_shape=jax.ShapeDtypeStruct((rows, width), jnp.bfloat16),
        in_specs=[SMEM] + [VMEM] * (2 + len(blocks)),
        out_specs=VMEM,
        scratch_shapes=[pltpu.VMEM((rows, width), jnp.bfloat16)],
        compiler_params=PARAMS,
        cost_estimate=cost(2.0),
    )(owner_groups, rotator, eigenvalues, *blocks)


def score_kernel(factor, mine_ref, other_ref, *refs):
    count = len(refs) // 2
    for pair, out in zip(refs[:count], refs[count:]):
        rows = out.shape[0]
        total = 0.0
        for half, asked in enumerate((mine_ref, other_ref)):
            total += lax.dot_general(
                pair[half * rows : (half + 1) * rows, :],
                asked[...],
                (((1,), (1,)), ((), ())),
                preferred_element_type=jnp.float32,
            )
        out[...] = factor * total


def score(mine, other, pairs, factor):
    part = jax.ShapeDtypeStruct((pairs[0].shape[0] // 2, mine.shape[0]), jnp.float32)
    return pl.pallas_call(
        functools.partial(score_kernel, factor),
        out_shape=(part,) * len(pairs),
        in_specs=[VMEM] * (2 + len(pairs)),
        out_specs=(VMEM,) * len(pairs),
        compiler_params=PARAMS,
        cost_estimate=cost(0.7),
    )(mine, other, *pairs)


def swap(array, axis, bits):
    return lax.ppermute(array, axis, [(i, i ^ bits) for i in range(lax.axis_size(axis))])


def after(array, *others):
    return lax.optimization_barrier((array,) + others)[0]


def local(train_grads, query_grads, basis_out, basis_in, eigenvalues, owner_groups, module_order):
    _, modules, width = train_grads.shape
    groups = lax.axis_size("group")
    inner = 1 << ((groups.bit_length() - 1) // 2)
    own = query_grads.reshape(-1, width)
    blocks = [None] * groups
    for far in reversed(range(inner, groups, inner)):
        blocks[far] = swap(own, "group", far)
    first = blocks[inner]
    blocks[0] = after(own, first)
    pairs = by_slot(module_order, after(train_grads, first))
    pairs = [pairs[0]] + [swap(pairs[j], "module", 2 * j) for j in range(1, modules // 2)]
    rotator = rotator_of(after(basis_out[0], first), basis_in[0])
    for far in range(0, groups, inner):
        if far > inner:
            blocks[far] = after(blocks[far], rotator)
        for near in range(1, inner):
            blocks[far + near] = swap(blocks[far], "group", near)
    mine = precondition(owner_groups, rotator, eigenvalues, blocks)
    other = swap(mine, "module", 1)
    parts = score(mine, other, pairs, 1.0 / math.sqrt(modules * width))
    total = parts[0]
    for j in range(1, modules // 2):
        total = total + swap(parts[j], "module", 2 * j)
    return total


def solution(mesh):
    in_specs = (
        P(("group", "module"), None, None),
        P("group", None, "module", None),
        P("module", None, None),
        P("module", None, None),
        P("module", None),
        P(),
        P(),
    )
    out_specs = P(("group", "module"), None)
    return jax.shard_map(local, mesh=mesh, in_specs=in_specs, out_specs=out_specs, check_vma=False)
```

```python
import functools
import math

import jax
import jax.numpy as jnp
from jax import lax
from jax.experimental import pallas as pl
from jax.experimental.pallas import tpu as pltpu
from jax.sharding import PartitionSpec as P

LANES = 128
VMEM = pl.BlockSpec(memory_space=pltpu.VMEM)
HBM = pl.BlockSpec(memory_space=pltpu.HBM)
PARAMS = pltpu.CompilerParams(vmem_limit_bytes=32 * 1024 * 1024)


def place_of(owners, k, me, inner):
    seen = [owners[j] ^ me for j in range(owners.shape[0])]
    near, far = seen[k] % inner, seen[k] // inner
    place = jnp.int32(0)
    for other in seen:
        place += jnp.logical_and(other % inner == near, other // inner < far).astype(jnp.int32)
    return near, far, place


def prepare_kernel(inner, each, order_hbm, owners_hbm, out_hbm, in_hbm, values_hbm, own_hbm, train_hbm, *refs):
    rotator_ref, inverse_ref, send_ref, pick_ref, own_ref, *pairs = refs[:-8]
    order, owners, out_ref, in_ref, values, train, wide, sems = refs[-8:]
    loads = [
        pltpu.make_async_copy(src, dst, sems.at[i])
        for i, (src, dst) in enumerate(
            (
                (out_hbm, out_ref),
                (in_hbm, in_ref),
                (order_hbm, order),
                (owners_hbm, owners),
                (values_hbm, values),
                (own_hbm, own_ref),
                (train_hbm, train),
            )
        )
    ]
    for load in loads:
        load.start()
    side, width = out_ref.shape[1], rotator_ref.shape[0]
    column = lax.broadcasted_iota(jnp.int32, (side, width), 1)
    row = lax.broadcasted_iota(jnp.int32, (side, width), 0)
    spread = (column // side == row).astype(jnp.bfloat16)
    tiled = (column % side == row).astype(jnp.bfloat16)
    for load in loads[:2]:
        load.wait()
    outer = jnp.dot(out_ref[0], spread, preferred_element_type=jnp.float32)
    inside = jnp.dot(in_ref[0], tiled, preferred_element_type=jnp.float32)
    for a in range(side):
        rotator_ref[pl.ds(a * side, side), :] = (outer[a : a + 1, :] * inside).astype(jnp.bfloat16)
    for load in loads[2:]:
        load.wait()
    spectrum = values[...]
    inverse_ref[...] = 1.0 / (spectrum + 0.1 * jnp.mean(spectrum, axis=1, keepdims=True))

    me = lax.axis_index("group")
    places = send_ref.shape[0] // each
    line = lax.broadcasted_iota(jnp.int32, send_ref.shape, 0)
    lane = lax.broadcasted_iota(jnp.int32, send_ref.shape, 1)
    send = jnp.zeros(send_ref.shape, jnp.float32)
    line_p = lax.broadcasted_iota(jnp.int32, pick_ref.shape, 0)
    lane_p = lax.broadcasted_iota(jnp.int32, pick_ref.shape, 1)
    pick = jnp.zeros(pick_ref.shape, jnp.float32)
    for k in range(owners.shape[0]):
        near, far, place = place_of(owners, k, me, inner)
        shift = jnp.where(near == 0, (far - place) * each, -2 * send_ref.shape[1])
        hit = jnp.logical_and(lane - line == shift, line // each == place)
        send = jnp.where(hit, 1.0, send)
        shift = (near * places + place - k) * each
        hit = jnp.logical_and(lane_p - line_p == shift, line_p // each == k)
        pick = jnp.where(hit, 1.0, pick)
    send_ref[...] = send.astype(jnp.bfloat16)
    pick_ref[...] = pick.astype(jnp.bfloat16)

    rows, modules, _ = train.shape
    tiles = width // LANES
    slot = lax.axis_index("module")
    for e in range(rows):
        example = train[e].astype(jnp.float32)
        for t in range(tiles):
            wide[pl.ds((t * rows + e) * modules, modules), :] = example[:, t * LANES : (t + 1) * LANES]
    for j in range(modules):
        held = order[slot ^ j]
        out, at = pairs[j // 2], j % 2 * rows
        for t in range(tiles):
            piece = wide[pl.ds(t * rows * modules + held, rows, stride=modules), :]
            out[at : at + rows, t * LANES : (t + 1) * LANES] = piece.astype(out.dtype)


def prepare(train_grads, own, basis_out, basis_in, eigenvalues, owner_groups, module_order, inner, blocks):
    each = own.shape[0]
    rows, modules, width = train_grads.shape
    asked = owner_groups.shape[0]
    places = min(blocks, asked - (inner > 1))
    pair = jax.ShapeDtypeStruct((2 * rows, width), train_grads.dtype)
    shapes = (
        jax.ShapeDtypeStruct((width, width), jnp.bfloat16),
        jax.ShapeDtypeStruct(eigenvalues.shape, jnp.float32),
        jax.ShapeDtypeStruct((places * each, blocks * each), jnp.bfloat16),
        jax.ShapeDtypeStruct((asked * each, inner * places * each), jnp.bfloat16),
        jax.ShapeDtypeStruct(own.shape, own.dtype),
    ) + (pair,) * (modules // 2)
    return pl.pallas_call(
        functools.partial(prepare_kernel, inner, each),
        out_shape=shapes,
        in_specs=[HBM] * 7,
        out_specs=(VMEM,) * len(shapes),
        scratch_shapes=[
            pltpu.SMEM(module_order.shape, jnp.int32),
            pltpu.SMEM(owner_groups.shape, jnp.int32),
            pltpu.VMEM(basis_out.shape, basis_out.dtype),
            pltpu.VMEM(basis_in.shape, basis_in.dtype),
            pltpu.VMEM(eigenvalues.shape, eigenvalues.dtype),
            pltpu.VMEM(train_grads.shape, train_grads.dtype),
            pltpu.VMEM((rows * modules * width // LANES, LANES), jnp.float32),
            pltpu.SemaphoreType.DMA((7,)),
        ],
        compiler_params=PARAMS,
    )(
        *(
            pltpu.with_memory_space_constraint(operand, pltpu.HBM)
            for operand in (module_order, owner_groups, basis_out, basis_in, eigenvalues, own, train_grads)
        )
    )


def precondition_kernel(send_ref, rotator_ref, inverse_ref, *refs):
    *blocks, out = refs
    each = blocks[0].shape[0]
    queries = 0.0
    for b, block in enumerate(blocks):
        queries += jnp.dot(
            send_ref[:, b * each : (b + 1) * each], block[...], preferred_element_type=jnp.float32
        )
    asked = inverse_ref[...] * jnp.dot(
        queries.astype(jnp.bfloat16), rotator_ref[...], preferred_element_type=jnp.float32
    )
    out[...] = lax.dot_general(
        asked.astype(jnp.bfloat16),
        rotator_ref[...],
        (((1,), (1,)), ((), ())),
        preferred_element_type=jnp.float32,
    ).astype(out.dtype)


def precondition(send, rotator, inverse, blocks):
    return pl.pallas_call(
        precondition_kernel,
        out_shape=jax.ShapeDtypeStruct((send.shape[0], rotator.shape[0]), jnp.bfloat16),
        in_specs=[VMEM] * (3 + len(blocks)),
        out_specs=VMEM,
        compiler_params=PARAMS,
    )(send, rotator, inverse, *blocks)


def score_kernel(inner, factor, pick_ref, *refs):
    columns, refs = refs[: 2 * inner], refs[2 * inner :]
    count = len(refs) // 2
    span = columns[0].shape[0]
    asked = []
    for half in range(2):
        chosen = 0.0
        for column in range(inner):
            chosen += jnp.dot(
                pick_ref[:, column * span : (column + 1) * span],
                columns[2 * column + half][...],
                preferred_element_type=jnp.float32,
            )
        asked.append(chosen.astype(jnp.bfloat16))
    for pair, out in zip(refs[:count], refs[count:]):
        rows = out.shape[0]
        total = 0.0
        for half in range(2):
            total += lax.dot_general(
                pair[half * rows : (half + 1) * rows, :],
                asked[half],
                (((1,), (1,)), ((), ())),
                preferred_element_type=jnp.float32,
            )
        out[...] = factor * total


def score(pick, columns, pairs, factor):
    part = jax.ShapeDtypeStruct((pairs[0].shape[0] // 2, pick.shape[0]), jnp.float32)
    return pl.pallas_call(
        functools.partial(score_kernel, len(columns) // 2, factor),
        out_shape=(part,) * len(pairs),
        in_specs=[VMEM] * (1 + len(columns) + len(pairs)),
        out_specs=(VMEM,) * len(pairs),
        compiler_params=PARAMS,
    )(pick, *columns, *pairs)


def swap(array, axis, bits):
    return lax.ppermute(array, axis, [(i, i ^ bits) for i in range(lax.axis_size(axis))])


def after(array, *others):
    return lax.optimization_barrier((array,) + others)[0]


def local(train_grads, query_grads, basis_out, basis_in, eigenvalues, owner_groups, module_order):
    _, modules, width = train_grads.shape
    groups = lax.axis_size("group")
    inner = 1 << ((groups.bit_length() - 1) // 2)
    own = query_grads.reshape(-1, width)
    each = own.shape[0]
    blocks = [own] + [swap(own, "group", far) for far in range(inner, groups, inner)]
    rotator, inverse, send, pick, own, *pairs = prepare(
        train_grads,
        own,
        basis_out,
        basis_in,
        eigenvalues,
        owner_groups,
        module_order,
        inner,
        len(blocks),
    )
    blocks[0] = own
    pairs = [pairs[0]] + [swap(pairs[j], "module", 2 * j) for j in range(1, modules // 2)]
    mine = precondition(send, rotator, inverse, blocks)
    columns = [mine, swap(mine, "module", 1)]
    for near in range(1, inner):
        theirs = swap(mine, "group", near)
        columns += [theirs, swap(after(theirs, *pairs), "module", 1)]
    parts = score(pick, columns, pairs, 1.0 / math.sqrt(modules * width))
    total = parts[0]
    for j in range(1, modules // 2):
        total = total + swap(parts[j], "module", 2 * j)
    return total


def solution(mesh):
    in_specs = (
        P(("group", "module"), None, None),
        P("group", None, "module", None),
        P("module", None, None),
        P("module", None, None),
        P("module", None),
        P(),
        P(),
    )
    out_specs = P(("group", "module"), None)
    return jax.shard_map(local, mesh=mesh, in_specs=in_specs, out_specs=out_specs, check_vma=False)
```

```python
import functools
import math

import jax
import jax.numpy as jnp
from jax import lax
from jax.experimental import pallas as pl
from jax.experimental.pallas import tpu as pltpu
from jax.sharding import PartitionSpec as P

LANES = 128
VMEM = pl.BlockSpec(memory_space=pltpu.VMEM)
HBM = pl.BlockSpec(memory_space=pltpu.HBM)
PARAMS = pltpu.CompilerParams(vmem_limit_bytes=32 * 1024 * 1024)


def place_of(owners, k, me, inner):
    seen = [owners[j] ^ me for j in range(owners.shape[0])]
    near, far = seen[k] % inner, seen[k] // inner
    place = jnp.int32(0)
    for other in seen:
        place += jnp.logical_and(other % inner == near, other // inner < far).astype(jnp.int32)
    return near, far, place


def build_rotator(basis_out, basis_in, rotator_ref):
    side, width = basis_out.shape[0], rotator_ref.shape[0]
    column = lax.broadcasted_iota(jnp.int32, (side, width), 1)
    row = lax.broadcasted_iota(jnp.int32, (side, width), 0)
    spread = (column // side == row).astype(jnp.bfloat16)
    tiled = (column % side == row).astype(jnp.bfloat16)
    outer = jnp.dot(basis_out, spread, preferred_element_type=jnp.float32)
    inside = jnp.dot(basis_in, tiled, preferred_element_type=jnp.float32)
    for a in range(side):
        rotator_ref[pl.ds(a * side, side), :] = (outer[a : a + 1, :] * inside).astype(jnp.bfloat16)


def prepare_kernel(inner, each, order_hbm, owners_hbm, out_hbm, in_hbm, values_hbm, own_hbm, train_hbm, *refs):
    rotator_ref, inverse_ref, send_ref, pick_ref, own_ref, bases_ref, *pairs = refs[:-8]
    order, owners, out_ref, in_ref, values, train, wide, sems = refs[-8:]
    loads = [
        pltpu.make_async_copy(src, dst, sems.at[i])
        for i, (src, dst) in enumerate(
            (
                (out_hbm, out_ref),
                (in_hbm, in_ref),
                (order_hbm, order),
                (owners_hbm, owners),
                (values_hbm, values),
                (own_hbm, own_ref),
                (train_hbm, train),
            )
        )
    ]
    for load in loads:
        load.start()
    side, width = out_ref.shape[1], rotator_ref.shape[0]
    for load in loads[:2]:
        load.wait()
    bases_ref[:side, :] = out_ref[0]
    bases_ref[side:, :] = in_ref[0]
    build_rotator(out_ref[0], in_ref[0], rotator_ref)
    for load in loads[2:]:
        load.wait()
    spectrum = values[...]
    inverse_ref[...] = 1.0 / (spectrum + 0.1 * jnp.mean(spectrum, axis=1, keepdims=True))

    me = lax.axis_index("group")
    places = send_ref.shape[0] // each
    line = lax.broadcasted_iota(jnp.int32, send_ref.shape, 0)
    lane = lax.broadcasted_iota(jnp.int32, send_ref.shape, 1)
    send = jnp.zeros(send_ref.shape, jnp.float32)
    line_p = lax.broadcasted_iota(jnp.int32, pick_ref.shape, 0)
    lane_p = lax.broadcasted_iota(jnp.int32, pick_ref.shape, 1)
    pick = jnp.zeros(pick_ref.shape, jnp.float32)
    for k in range(owners.shape[0]):
        near, far, place = place_of(owners, k, me, inner)
        shift = jnp.where(near == 0, (far - place) * each, -2 * send_ref.shape[1])
        hit = jnp.logical_and(lane - line == shift, line // each == place)
        send = jnp.where(hit, 1.0, send)
        shift = (near * places + place - k) * each
        hit = jnp.logical_and(lane_p - line_p == shift, line_p // each == k)
        pick = jnp.where(hit, 1.0, pick)
    send_ref[...] = send.astype(jnp.bfloat16)
    pick_ref[...] = pick.astype(jnp.bfloat16)

    rows, modules, _ = train.shape
    tiles = width // LANES
    slot = lax.axis_index("module")
    for e in range(rows):
        example = train[e].astype(jnp.float32)
        for t in range(tiles):
            wide[pl.ds((t * rows + e) * modules, modules), :] = example[:, t * LANES : (t + 1) * LANES]
    for j in range(modules):
        held = order[slot ^ j]
        out, at = pairs[j // 2], j % 2 * rows
        for t in range(tiles):
            piece = wide[pl.ds(t * rows * modules + held, rows, stride=modules), :]
            out[at : at + rows, t * LANES : (t + 1) * LANES] = piece.astype(out.dtype)


def prepare(train_grads, own, basis_out, basis_in, eigenvalues, owner_groups, module_order, inner, blocks):
    each = own.shape[0]
    rows, modules, width = train_grads.shape
    asked = owner_groups.shape[0]
    places = min(blocks, asked - (inner > 1))
    pair = jax.ShapeDtypeStruct((2 * rows, width), train_grads.dtype)
    shapes = (
        jax.ShapeDtypeStruct((width, width), jnp.bfloat16),
        jax.ShapeDtypeStruct(eigenvalues.shape, jnp.float32),
        jax.ShapeDtypeStruct((places * each, blocks * each), jnp.bfloat16),
        jax.ShapeDtypeStruct((asked * each, inner * places * each), jnp.bfloat16),
        jax.ShapeDtypeStruct(own.shape, own.dtype),
        jax.ShapeDtypeStruct((2 * basis_out.shape[1], basis_out.shape[2]), basis_out.dtype),
    ) + (pair,) * (modules // 2)
    return pl.pallas_call(
        functools.partial(prepare_kernel, inner, each),
        out_shape=shapes,
        in_specs=[HBM] * 7,
        out_specs=(VMEM,) * len(shapes),
        scratch_shapes=[
            pltpu.SMEM(module_order.shape, jnp.int32),
            pltpu.SMEM(owner_groups.shape, jnp.int32),
            pltpu.VMEM(basis_out.shape, basis_out.dtype),
            pltpu.VMEM(basis_in.shape, basis_in.dtype),
            pltpu.VMEM(eigenvalues.shape, eigenvalues.dtype),
            pltpu.VMEM(train_grads.shape, train_grads.dtype),
            pltpu.VMEM((rows * modules * width // LANES, LANES), jnp.float32),
            pltpu.SemaphoreType.DMA((7,)),
        ],
        compiler_params=PARAMS,
    )(
        *(
            pltpu.with_memory_space_constraint(operand, pltpu.HBM)
            for operand in (module_order, owner_groups, basis_out, basis_in, eigenvalues, own, train_grads)
        )
    )


def ask_kernel(order, send_ref, rotator_ref, inverse_ref, *refs):
    *blocks, out = refs
    each = blocks[0].shape[0]
    queries = 0.0
    for b, block in zip(order, blocks):
        queries += jnp.dot(
            send_ref[:, b * each : (b + 1) * each], block[...], preferred_element_type=jnp.float32
        )
    out[...] = (
        inverse_ref[...]
        * jnp.dot(queries.astype(jnp.bfloat16), rotator_ref[...], preferred_element_type=jnp.float32)
    ).astype(out.dtype)


def ask(send, rotator, inverse, blocks):
    order = (*range(2, len(blocks)), 1, 0)
    return pl.pallas_call(
        functools.partial(ask_kernel, order),
        out_shape=jax.ShapeDtypeStruct((send.shape[0], rotator.shape[0]), jnp.bfloat16),
        in_specs=[VMEM] * (3 + len(blocks)),
        out_specs=VMEM,
        compiler_params=PARAMS,
    )(send, rotator, inverse, *(blocks[b] for b in order))


def turn_kernel(bases_ref, rotator_ref, pair, other_ref, turned):
    rows, side = pair.shape[0] // 2, bases_ref.shape[1]
    build_rotator(bases_ref[:side, :], bases_ref[side:, :], other_ref)
    turn_pair(rows, pair, rotator_ref, other_ref, turned)


def turn_pair(rows, pair, rotator_ref, other_ref, turned):
    for half, rotator in enumerate((rotator_ref, other_ref)):
        at = slice(half * rows, (half + 1) * rows)
        turned[at, :] = jnp.dot(
            pair[at, :], rotator[...], preferred_element_type=jnp.float32
        ).astype(turned.dtype)


def turn_more_kernel(rotator_ref, other_ref, *refs):
    count = len(refs) // 2
    for pair, turned in zip(refs[:count], refs[count:]):
        turn_pair(pair.shape[0] // 2, pair, rotator_ref, other_ref, turned)


def turn(bases, rotator, pair):
    return pl.pallas_call(
        turn_kernel,
        out_shape=(
            jax.ShapeDtypeStruct(rotator.shape, rotator.dtype),
            jax.ShapeDtypeStruct(pair.shape, pair.dtype),
        ),
        in_specs=[VMEM] * 3,
        out_specs=(VMEM,) * 2,
        compiler_params=PARAMS,
    )(bases, rotator, pair)


def turn_more(rotator, other, pairs):
    return pl.pallas_call(
        turn_more_kernel,
        out_shape=tuple(jax.ShapeDtypeStruct(pair.shape, pair.dtype) for pair in pairs),
        in_specs=[VMEM] * (2 + len(pairs)),
        out_specs=(VMEM,) * len(pairs),
        compiler_params=PARAMS,
    )(rotator, other, *pairs)


def score_kernel(inner, factor, pick_ref, *refs):
    columns, refs = refs[: 2 * inner], refs[2 * inner :]
    pairs, outs = refs[: len(refs) // 2], refs[len(refs) // 2 :]
    span, rows = columns[0].shape[0], outs[0].shape[0]
    total = 0.0
    for half in range(2):
        asked = 0.0
        for column in range(inner):
            asked += jnp.dot(
                pick_ref[:, column * span : (column + 1) * span],
                columns[2 * column + half][...],
                preferred_element_type=jnp.float32,
            )
        turned = [pair[half * rows : (half + 1) * rows, :] for pair in pairs]
        total += lax.dot_general(
            jnp.concatenate(turned, axis=0),
            asked.astype(jnp.bfloat16),
            (((1,), (1,)), ((), ())),
            preferred_element_type=jnp.float32,
        )
    for j, out in enumerate(outs):
        out[...] = factor * total[j * rows : (j + 1) * rows, :]


def score(pick, columns, pairs, factor):
    part = jax.ShapeDtypeStruct((pairs[0].shape[0] // 2, pick.shape[0]), jnp.float32)
    return pl.pallas_call(
        functools.partial(score_kernel, len(columns) // 2, factor),
        out_shape=(part,) * len(pairs),
        in_specs=[VMEM] * (1 + len(columns) + len(pairs)),
        out_specs=(VMEM,) * len(pairs),
        compiler_params=PARAMS,
    )(pick, *columns, *pairs)


def swap(array, axis, bits):
    return lax.ppermute(array, axis, [(i, i ^ bits) for i in range(lax.axis_size(axis))])


def after(array, *others):
    return lax.optimization_barrier((array,) + others)[0]


def local(train_grads, query_grads, basis_out, basis_in, eigenvalues, owner_groups, module_order):
    _, modules, width = train_grads.shape
    groups = lax.axis_size("group")
    inner = 1 << ((groups.bit_length() - 1) // 2)
    own = query_grads.reshape(-1, width)
    each = own.shape[0]
    blocks = [own] + [swap(own, "group", far) for far in range(inner, groups, inner)]
    rotator, inverse, send, pick, own, bases, *pairs = prepare(
        train_grads,
        own,
        basis_out,
        basis_in,
        eigenvalues,
        owner_groups,
        module_order,
        inner,
        len(blocks),
    )
    blocks[0] = own
    sent = [swap(pairs[j], "module", 2 * j) for j in range(1, modules // 2)]
    mine = ask(send, rotator, inverse, blocks)
    other, turned = turn(after(swap(bases, "module", 1), mine), rotator, pairs[0])
    turned = [turned, *turn_more(rotator, other, sent)]
    columns = [mine, swap(mine, "module", 1)]
    for near in range(1, inner):
        theirs = swap(mine, "group", near)
        columns += [theirs, swap(after(theirs, *turned), "module", 1)]
    parts = score(pick, columns, turned, 1.0 / math.sqrt(modules * width))
    total = parts[0]
    for j in range(1, modules // 2):
        total = total + swap(parts[j], "module", 2 * j)
    return total


def solution(mesh):
    in_specs = (
        P(("group", "module"), None, None),
        P("group", None, "module", None),
        P("module", None, None),
        P("module", None, None),
        P("module", None),
        P(),
        P(),
    )
    out_specs = P(("group", "module"), None)
    return jax.shard_map(local, mesh=mesh, in_specs=in_specs, out_specs=out_specs, check_vma=False)
```

```python
import functools
import math

import jax
import jax.numpy as jnp
from jax import lax
from jax.experimental import pallas as pl
from jax.experimental.pallas import tpu as pltpu
from jax.sharding import PartitionSpec as P

LANES = 128
VMEM = pl.BlockSpec(memory_space=pltpu.VMEM)
HBM = pl.BlockSpec(memory_space=pltpu.HBM)
PARAMS = pltpu.CompilerParams(vmem_limit_bytes=32 * 1024 * 1024)


def place_of(owners, k, me, inner):
    seen = [owners[j] ^ me for j in range(owners.shape[0])]
    near, far = seen[k] % inner, seen[k] // inner
    place = jnp.int32(0)
    for other in seen:
        place += jnp.logical_and(other % inner == near, other // inner < far).astype(jnp.int32)
    return near, far, place


def build_rotator(basis_out, basis_in, rotator_ref):
    side, width = basis_out.shape[0], rotator_ref.shape[0]
    column = lax.broadcasted_iota(jnp.int32, (side, width), 1)
    row = lax.broadcasted_iota(jnp.int32, (side, width), 0)
    spread = (column // side == row).astype(jnp.bfloat16)
    tiled = (column % side == row).astype(jnp.bfloat16)
    outer = jnp.dot(basis_out, spread, preferred_element_type=jnp.float32)
    inside = jnp.dot(basis_in, tiled, preferred_element_type=jnp.float32)
    for a in range(side):
        rotator_ref[pl.ds(a * side, side), :] = (outer[a : a + 1, :] * inside).astype(jnp.bfloat16)


def prepare_kernel(inner, each, order_hbm, owners_hbm, out_hbm, in_hbm, values_hbm, own_hbm, train_hbm, *refs):
    rotator_ref, inverse_ref, send_ref, pick_ref, own_ref, bases_ref, *pairs = refs[:-8]
    order, owners, out_ref, in_ref, values, train, wide, sems = refs[-8:]
    loads = [
        pltpu.make_async_copy(src, dst, sems.at[i])
        for i, (src, dst) in enumerate(
            (
                (out_hbm, out_ref),
                (in_hbm, in_ref),
                (order_hbm, order),
                (owners_hbm, owners),
                (values_hbm, values),
                (own_hbm, own_ref),
                (train_hbm, train),
            )
        )
    ]
    for load in loads:
        load.start()
    side, width = out_ref.shape[1], rotator_ref.shape[0]
    for load in loads[:2]:
        load.wait()
    bases_ref[:side, :] = out_ref[0]
    bases_ref[side:, :] = in_ref[0]
    build_rotator(out_ref[0], in_ref[0], rotator_ref)
    for load in loads[2:]:
        load.wait()
    spectrum = values[...]
    inverse_ref[...] = 1.0 / (spectrum + 0.1 * jnp.mean(spectrum, axis=1, keepdims=True))

    me = lax.axis_index("group")
    places = send_ref.shape[0] // each
    line = lax.broadcasted_iota(jnp.int32, send_ref.shape, 0)
    lane = lax.broadcasted_iota(jnp.int32, send_ref.shape, 1)
    send = jnp.zeros(send_ref.shape, jnp.float32)
    line_p = lax.broadcasted_iota(jnp.int32, pick_ref.shape, 0)
    lane_p = lax.broadcasted_iota(jnp.int32, pick_ref.shape, 1)
    pick = jnp.zeros(pick_ref.shape, jnp.float32)
    for k in range(owners.shape[0]):
        near, far, place = place_of(owners, k, me, inner)
        shift = jnp.where(near == 0, (far - place) * each, -2 * send_ref.shape[1])
        hit = jnp.logical_and(lane - line == shift, line // each == place)
        send = jnp.where(hit, 1.0, send)
        shift = (near * places + place - k) * each
        hit = jnp.logical_and(lane_p - line_p == shift, line_p // each == k)
        pick = jnp.where(hit, 1.0, pick)
    send_ref[...] = send.astype(jnp.bfloat16)
    pick_ref[...] = pick.astype(jnp.bfloat16)

    rows, modules, _ = train.shape
    tiles = width // LANES
    slot = lax.axis_index("module")
    for e in range(rows):
        example = train[e].astype(jnp.float32)
        for t in range(tiles):
            wide[pl.ds((t * rows + e) * modules, modules), :] = example[:, t * LANES : (t + 1) * LANES]
    for j in range(modules):
        held = order[slot ^ j]
        out, at = pairs[j // 2], j % 2 * rows
        for t in range(tiles):
            piece = wide[pl.ds(t * rows * modules + held, rows, stride=modules), :]
            out[at : at + rows, t * LANES : (t + 1) * LANES] = piece.astype(out.dtype)


def prepare(train_grads, own, basis_out, basis_in, eigenvalues, owner_groups, module_order, inner, blocks):
    each = own.shape[0]
    rows, modules, width = train_grads.shape
    asked = owner_groups.shape[0]
    places = min(blocks, asked - (inner > 1))
    pair = jax.ShapeDtypeStruct((2 * rows, width), train_grads.dtype)
    shapes = (
        jax.ShapeDtypeStruct((width, width), jnp.bfloat16),
        jax.ShapeDtypeStruct(eigenvalues.shape, jnp.float32),
        jax.ShapeDtypeStruct((places * each, blocks * each), jnp.bfloat16),
        jax.ShapeDtypeStruct((asked * each, inner * places * each), jnp.bfloat16),
        jax.ShapeDtypeStruct(own.shape, own.dtype),
        jax.ShapeDtypeStruct((2 * basis_out.shape[1], basis_out.shape[2]), basis_out.dtype),
    ) + (pair,) * (modules // 2)
    return pl.pallas_call(
        functools.partial(prepare_kernel, inner, each),
        out_shape=shapes,
        in_specs=[HBM] * 7,
        out_specs=(VMEM,) * len(shapes),
        scratch_shapes=[
            pltpu.SMEM(module_order.shape, jnp.int32),
            pltpu.SMEM(owner_groups.shape, jnp.int32),
            pltpu.VMEM(basis_out.shape, basis_out.dtype),
            pltpu.VMEM(basis_in.shape, basis_in.dtype),
            pltpu.VMEM(eigenvalues.shape, eigenvalues.dtype),
            pltpu.VMEM(train_grads.shape, train_grads.dtype),
            pltpu.VMEM((rows * modules * width // LANES, LANES), jnp.float32),
            pltpu.SemaphoreType.DMA((7,)),
        ],
        compiler_params=PARAMS,
    )(
        *(
            pltpu.with_memory_space_constraint(operand, pltpu.HBM)
            for operand in (module_order, owner_groups, basis_out, basis_in, eigenvalues, own, train_grads)
        )
    )


def ask_kernel(order, send_ref, rotator_ref, inverse_ref, *refs):
    *blocks, out = refs
    queries = jnp.dot(
        send_ref[...],
        jnp.concatenate([blocks[order.index(b)][...] for b in range(len(order))], axis=0),
        preferred_element_type=jnp.float32,
    )
    out[...] = (
        inverse_ref[...]
        * jnp.dot(queries.astype(jnp.bfloat16), rotator_ref[...], preferred_element_type=jnp.float32)
    ).astype(out.dtype)


def ask(send, rotator, inverse, blocks):
    order = (*range(2, len(blocks)), 1, 0)
    return pl.pallas_call(
        functools.partial(ask_kernel, order),
        out_shape=jax.ShapeDtypeStruct((send.shape[0], rotator.shape[0]), jnp.bfloat16),
        in_specs=[VMEM] * (3 + len(blocks)),
        out_specs=VMEM,
        compiler_params=PARAMS,
    )(send, rotator, inverse, *(blocks[b] for b in order))


def turn_kernel(bases_ref, rotator_ref, pair, other_ref, turned):
    rows, side = pair.shape[0] // 2, bases_ref.shape[1]
    build_rotator(bases_ref[:side, :], bases_ref[side:, :], other_ref)
    turn_pair(rows, pair, rotator_ref, other_ref, turned)


def turn_pair(rows, pair, rotator_ref, other_ref, turned):
    for half, rotator in enumerate((rotator_ref, other_ref)):
        at = slice(half * rows, (half + 1) * rows)
        turned[at, :] = jnp.dot(
            pair[at, :], rotator[...], preferred_element_type=jnp.float32
        ).astype(turned.dtype)


def turn_more_kernel(rotator_ref, other_ref, *refs):
    count = len(refs) // 2
    for pair, turned in zip(refs[:count], refs[count:]):
        turn_pair(pair.shape[0] // 2, pair, rotator_ref, other_ref, turned)


def turn(bases, rotator, pair):
    return pl.pallas_call(
        turn_kernel,
        out_shape=(
            jax.ShapeDtypeStruct(rotator.shape, rotator.dtype),
            jax.ShapeDtypeStruct(pair.shape, pair.dtype),
        ),
        in_specs=[VMEM] * 3,
        out_specs=(VMEM,) * 2,
        compiler_params=PARAMS,
    )(bases, rotator, pair)


def turn_more(rotator, other, pairs):
    return pl.pallas_call(
        turn_more_kernel,
        out_shape=tuple(jax.ShapeDtypeStruct(pair.shape, pair.dtype) for pair in pairs),
        in_specs=[VMEM] * (2 + len(pairs)),
        out_specs=(VMEM,) * len(pairs),
        compiler_params=PARAMS,
    )(rotator, other, *pairs)


def add_scores(total, pick_ref, columns, half, pairs):
    span, rows = columns[0][1].shape[0], pairs[0].shape[0] // 2
    first, last = columns[0][0], columns[-1][0]
    asked = jnp.dot(
        pick_ref[:, first * span : (last + 1) * span],
        jnp.concatenate([places[...] for _, places in columns], axis=0),
        preferred_element_type=jnp.float32,
    )
    turned = [pair[half * rows : (half + 1) * rows, :] for pair in pairs]
    return total + lax.dot_general(
        jnp.concatenate(turned, axis=0),
        asked.astype(jnp.bfloat16),
        (((1,), (1,)), ((), ())),
        preferred_element_type=jnp.float32,
    )


def early_kernel(inner, pick_ref, *refs):
    asked, pairs, out = refs[: inner + 1], refs[inner + 1 : -1], refs[-1]
    total = add_scores(0.0, pick_ref, list(enumerate(asked[:inner])), 0, pairs)
    out[...] = add_scores(total, pick_ref, [(0, asked[inner])], 1, pairs)


def late_kernel(inner, factor, pick_ref, early_ref, *refs):
    asked, refs = refs[: inner - 1], refs[inner - 1 :]
    pairs, outs = refs[: len(refs) // 2], refs[len(refs) // 2 :]
    total = add_scores(early_ref[...], pick_ref, list(enumerate(asked, 1)), 1, pairs)
    rows = outs[0].shape[0]
    for j, out in enumerate(outs):
        out[...] = factor * total[j * rows : (j + 1) * rows, :]


def score(pick, mine, others, turned, factor):
    inner = 1 + len(others)
    rows = turned[0].shape[0] // 2
    early = pl.pallas_call(
        functools.partial(early_kernel, inner),
        out_shape=jax.ShapeDtypeStruct((len(turned) * rows, pick.shape[0]), jnp.float32),
        in_specs=[VMEM] * (2 + inner + len(turned)),
        out_specs=VMEM,
        compiler_params=PARAMS,
    )(pick, mine[0], *(own for own, _ in others), mine[1], *turned)
    part = jax.ShapeDtypeStruct((rows, pick.shape[0]), jnp.float32)
    return pl.pallas_call(
        functools.partial(late_kernel, inner, factor),
        out_shape=(part,) * len(turned),
        in_specs=[VMEM] * (1 + inner + len(turned)),
        out_specs=(VMEM,) * len(turned),
        compiler_params=PARAMS,
    )(pick, early, *(other for _, other in others), *turned)


def swap(array, axis, bits):
    return lax.ppermute(array, axis, [(i, i ^ bits) for i in range(lax.axis_size(axis))])


def after(array, *others):
    return lax.optimization_barrier((array,) + others)[0]


def local(train_grads, query_grads, basis_out, basis_in, eigenvalues, owner_groups, module_order):
    _, modules, width = train_grads.shape
    groups = lax.axis_size("group")
    inner = 1 << ((groups.bit_length() - 1) // 2)
    own = query_grads.reshape(-1, width)
    each = own.shape[0]
    blocks = [own] + [swap(own, "group", far) for far in range(inner, groups, inner)]
    rotator, inverse, send, pick, own, bases, *pairs = prepare(
        train_grads,
        own,
        basis_out,
        basis_in,
        eigenvalues,
        owner_groups,
        module_order,
        inner,
        len(blocks),
    )
    blocks[0] = own
    sent = [swap(pairs[j], "module", 2 * j) for j in range(1, modules // 2)]
    mine = ask(send, rotator, inverse, blocks)
    other, turned = turn(after(swap(bases, "module", 1), mine), rotator, pairs[0])
    turned = [turned, *turn_more(rotator, other, sent)]
    theirs = [swap(mine, "group", near) for near in range(1, inner)]
    others = [(own, swap(after(own, *turned), "module", 1)) for own in theirs]
    factor = 1.0 / math.sqrt(modules * width)
    parts = score(pick, (mine, swap(mine, "module", 1)), others, turned, factor)
    total = parts[0]
    for j in range(1, modules // 2):
        total = total + swap(parts[j], "module", 2 * j)
    return total


def solution(mesh):
    in_specs = (
        P(("group", "module"), None, None),
        P("group", None, "module", None),
        P("module", None, None),
        P("module", None, None),
        P("module", None),
        P(),
        P(),
    )
    out_specs = P(("group", "module"), None)
    return jax.shard_map(local, mesh=mesh, in_specs=in_specs, out_specs=out_specs, check_vma=False)
```

```python
import functools
import math

import jax
import jax.numpy as jnp
from jax import lax
from jax.experimental import pallas as pl
from jax.experimental.pallas import tpu as pltpu
from jax.sharding import PartitionSpec as P

LANES = 128
VMEM = pl.BlockSpec(memory_space=pltpu.VMEM)
HBM = pl.BlockSpec(memory_space=pltpu.HBM)
PARAMS = pltpu.CompilerParams(vmem_limit_bytes=32 * 1024 * 1024)


def place_of(owners, k, me, inner):
    seen = [owners[j] ^ me for j in range(owners.shape[0])]
    near, far = seen[k] % inner, seen[k] // inner
    place = jnp.int32(0)
    for other in seen:
        place += jnp.logical_and(other % inner == near, other // inner < far).astype(jnp.int32)
    return near, far, place


def build_rotator(basis_out, basis_in, rotator_ref):
    side, width = basis_out.shape[0], rotator_ref.shape[0]
    column = lax.broadcasted_iota(jnp.int32, (side, width), 1)
    row = lax.broadcasted_iota(jnp.int32, (side, width), 0)
    spread = (column // side == row).astype(jnp.bfloat16)
    tiled = (column % side == row).astype(jnp.bfloat16)
    outer = jnp.dot(basis_out, spread, preferred_element_type=jnp.float32)
    inside = jnp.dot(basis_in, tiled, preferred_element_type=jnp.float32)
    for a in range(side):
        rotator_ref[pl.ds(a * side, side), :] = (outer[a : a + 1, :] * inside).astype(jnp.bfloat16)


def prepare_kernel(inner, each, order_hbm, owners_hbm, out_hbm, in_hbm, values_hbm, own_hbm, train_hbm, *refs):
    rotator_ref, inverse_ref, send_ref, pick_ref, own_ref, bases_ref, *pairs = refs[:-8]
    order, owners, out_ref, in_ref, values, train, wide, sems = refs[-8:]
    loads = [
        pltpu.make_async_copy(src, dst, sems.at[i])
        for i, (src, dst) in enumerate(
            (
                (out_hbm, out_ref),
                (in_hbm, in_ref),
                (order_hbm, order),
                (owners_hbm, owners),
                (values_hbm, values),
                (own_hbm, own_ref),
                (train_hbm, train),
            )
        )
    ]
    for load in loads:
        load.start()
    side, width = out_ref.shape[1], rotator_ref.shape[0]
    for load in loads[:2]:
        load.wait()
    bases_ref[:side, :] = out_ref[0]
    bases_ref[side:, :] = in_ref[0]
    build_rotator(out_ref[0], in_ref[0], rotator_ref)
    for load in loads[2:]:
        load.wait()
    spectrum = values[...]
    inverse_ref[...] = 1.0 / (spectrum + 0.1 * jnp.mean(spectrum, axis=1, keepdims=True))

    me = lax.axis_index("group")
    places = send_ref.shape[0] // each
    line = lax.broadcasted_iota(jnp.int32, send_ref.shape, 0)
    lane = lax.broadcasted_iota(jnp.int32, send_ref.shape, 1)
    send = jnp.zeros(send_ref.shape, jnp.float32)
    line_p = lax.broadcasted_iota(jnp.int32, pick_ref.shape, 0)
    lane_p = lax.broadcasted_iota(jnp.int32, pick_ref.shape, 1)
    pick = jnp.zeros(pick_ref.shape, jnp.float32)
    for k in range(owners.shape[0]):
        near, far, place = place_of(owners, k, me, inner)
        shift = jnp.where(near == 0, (far - place) * each, -2 * send_ref.shape[1])
        hit = jnp.logical_and(lane - line == shift, line // each == place)
        send = jnp.where(hit, 1.0, send)
        shift = (near * places + place - k) * each
        hit = jnp.logical_and(lane_p - line_p == shift, line_p // each == k)
        pick = jnp.where(hit, 1.0, pick)
    send_ref[...] = send.astype(jnp.bfloat16)
    pick_ref[...] = pick.astype(jnp.bfloat16)

    rows, modules, _ = train.shape
    tiles = width // LANES
    slot = lax.axis_index("module")
    for e in range(rows):
        example = train[e].astype(jnp.float32)
        for t in range(tiles):
            wide[pl.ds((t * rows + e) * modules, modules), :] = example[:, t * LANES : (t + 1) * LANES]
    for j in range(modules):
        held = order[slot ^ j]
        out, at = pairs[j // 2], j % 2 * rows
        for t in range(tiles):
            piece = wide[pl.ds(t * rows * modules + held, rows, stride=modules), :]
            out[at : at + rows, t * LANES : (t + 1) * LANES] = piece.astype(out.dtype)


def prepare(train_grads, own, basis_out, basis_in, eigenvalues, owner_groups, module_order, inner, blocks):
    each = own.shape[0]
    rows, modules, width = train_grads.shape
    asked = owner_groups.shape[0]
    places = min(blocks, asked - (inner > 1))
    pair = jax.ShapeDtypeStruct((2 * rows, width), train_grads.dtype)
    shapes = (
        jax.ShapeDtypeStruct((width, width), jnp.bfloat16),
        jax.ShapeDtypeStruct(eigenvalues.shape, jnp.float32),
        jax.ShapeDtypeStruct((places * each, blocks * each), jnp.bfloat16),
        jax.ShapeDtypeStruct((asked * each, inner * places * each), jnp.bfloat16),
        jax.ShapeDtypeStruct(own.shape, own.dtype),
        jax.ShapeDtypeStruct((2 * basis_out.shape[1], basis_out.shape[2]), basis_out.dtype),
    ) + (pair,) * (modules // 2)
    return pl.pallas_call(
        functools.partial(prepare_kernel, inner, each),
        out_shape=shapes,
        in_specs=[HBM] * 7,
        out_specs=(VMEM,) * len(shapes),
        scratch_shapes=[
            pltpu.SMEM(module_order.shape, jnp.int32),
            pltpu.SMEM(owner_groups.shape, jnp.int32),
            pltpu.VMEM(basis_out.shape, basis_out.dtype),
            pltpu.VMEM(basis_in.shape, basis_in.dtype),
            pltpu.VMEM(eigenvalues.shape, eigenvalues.dtype),
            pltpu.VMEM(train_grads.shape, train_grads.dtype),
            pltpu.VMEM((rows * modules * width // LANES + modules, LANES), jnp.float32),
            pltpu.SemaphoreType.DMA((7,)),
        ],
        compiler_params=PARAMS,
    )(
        *(
            pltpu.with_memory_space_constraint(operand, pltpu.HBM)
            for operand in (module_order, owner_groups, basis_out, basis_in, eigenvalues, own, train_grads)
        )
    )


def ask_kernel(order, send_ref, rotator_ref, inverse_ref, *refs):
    *blocks, out = refs
    queries = jnp.dot(
        send_ref[...],
        jnp.concatenate([blocks[order.index(b)][...] for b in range(len(order))], axis=0),
        preferred_element_type=jnp.float32,
    )
    out[...] = (
        inverse_ref[...]
        * jnp.dot(queries.astype(jnp.bfloat16), rotator_ref[...], preferred_element_type=jnp.float32)
    ).astype(out.dtype)


def ask(send, rotator, inverse, blocks):
    order = (*range(2, len(blocks)), 1, 0)
    return pl.pallas_call(
        functools.partial(ask_kernel, order),
        out_shape=jax.ShapeDtypeStruct((send.shape[0], rotator.shape[0]), jnp.bfloat16),
        in_specs=[VMEM] * (3 + len(blocks)),
        out_specs=VMEM,
        compiler_params=PARAMS,
    )(send, rotator, inverse, *(blocks[b] for b in order))


def turn_kernel(bases_ref, rotator_ref, pair, other_ref, turned):
    rows, side = pair.shape[0] // 2, bases_ref.shape[1]
    build_rotator(bases_ref[:side, :], bases_ref[side:, :], other_ref)
    turn_pair(rows, pair, rotator_ref, other_ref, turned)


def turn_pair(rows, pair, rotator_ref, other_ref, turned):
    for half, rotator in enumerate((rotator_ref, other_ref)):
        at = slice(half * rows, (half + 1) * rows)
        turned[at, :] = jnp.dot(
            pair[at, :], rotator[...], preferred_element_type=jnp.float32
        ).astype(turned.dtype)


def turn_more_kernel(rotator_ref, other_ref, *refs):
    count = len(refs) // 2
    for pair, turned in zip(refs[:count], refs[count:]):
        turn_pair(pair.shape[0] // 2, pair, rotator_ref, other_ref, turned)


def turn(bases, rotator, pair):
    return pl.pallas_call(
        turn_kernel,
        out_shape=(
            jax.ShapeDtypeStruct(rotator.shape, rotator.dtype),
            jax.ShapeDtypeStruct(pair.shape, pair.dtype),
        ),
        in_specs=[VMEM] * 3,
        out_specs=(VMEM,) * 2,
        compiler_params=PARAMS,
    )(bases, rotator, pair)


def turn_more(rotator, other, pairs):
    return pl.pallas_call(
        turn_more_kernel,
        out_shape=tuple(jax.ShapeDtypeStruct(pair.shape, pair.dtype) for pair in pairs),
        in_specs=[VMEM] * (2 + len(pairs)),
        out_specs=(VMEM,) * len(pairs),
        compiler_params=PARAMS,
    )(rotator, other, *pairs)


def add_scores(total, pick_ref, columns, half, pairs):
    span, rows = columns[0][1].shape[0], pairs[0].shape[0] // 2
    first, last = columns[0][0], columns[-1][0]
    asked = jnp.dot(
        pick_ref[:, first * span : (last + 1) * span],
        jnp.concatenate([places[...] for _, places in columns], axis=0),
        preferred_element_type=jnp.float32,
    )
    turned = [pair[half * rows : (half + 1) * rows, :] for pair in pairs]
    return total + lax.dot_general(
        jnp.concatenate(turned, axis=0),
        asked.astype(jnp.bfloat16),
        (((1,), (1,)), ((), ())),
        preferred_element_type=jnp.float32,
    )


def early_kernel(inner, pick_ref, *refs):
    asked, pairs, out = refs[: inner + 1], refs[inner + 1 : -1], refs[-1]
    total = add_scores(0.0, pick_ref, list(enumerate(asked[:inner])), 0, pairs)
    out[...] = add_scores(total, pick_ref, [(0, asked[inner])], 1, pairs)


def late_kernel(inner, factor, pick_ref, early_ref, *refs):
    asked, refs = refs[: inner - 1], refs[inner - 1 :]
    pairs, outs = refs[: len(refs) // 2], refs[len(refs) // 2 :]
    total = add_scores(early_ref[...], pick_ref, list(enumerate(asked, 1)), 1, pairs)
    rows = outs[0].shape[0]
    for j, out in enumerate(outs):
        out[...] = factor * total[j * rows : (j + 1) * rows, :]


def score(pick, mine, others, turned, factor):
    inner = 1 + len(others)
    rows = turned[0].shape[0] // 2
    early = pl.pallas_call(
        functools.partial(early_kernel, inner),
        out_shape=jax.ShapeDtypeStruct((len(turned) * rows, pick.shape[0]), jnp.float32),
        in_specs=[VMEM] * (2 + inner + len(turned)),
        out_specs=VMEM,
        compiler_params=PARAMS,
    )(pick, mine[0], *(own for own, _ in others), mine[1], *turned)
    part = jax.ShapeDtypeStruct((rows, pick.shape[0]), jnp.float32)
    return pl.pallas_call(
        functools.partial(late_kernel, inner, factor),
        out_shape=(part,) * len(turned),
        in_specs=[VMEM] * (1 + inner + len(turned)),
        out_specs=(VMEM,) * len(turned),
        compiler_params=PARAMS,
    )(pick, early, *(other for _, other in others), *turned)


def swap(array, axis, bits):
    return lax.ppermute(array, axis, [(i, i ^ bits) for i in range(lax.axis_size(axis))])


def after(array, *others):
    return lax.optimization_barrier((array,) + others)[0]


def local(train_grads, query_grads, basis_out, basis_in, eigenvalues, owner_groups, module_order):
    _, modules, width = train_grads.shape
    groups = lax.axis_size("group")
    inner = 1 << ((groups.bit_length() - 1) // 2)
    own = query_grads.reshape(-1, width)
    each = own.shape[0]
    blocks = [own] + [swap(own, "group", far) for far in range(inner, groups, inner)]
    rotator, inverse, send, pick, own, bases, *pairs = prepare(
        train_grads,
        own,
        basis_out,
        basis_in,
        eigenvalues,
        owner_groups,
        module_order,
        inner,
        len(blocks),
    )
    blocks[0] = own
    sent = [swap(pairs[j], "module", 2 * j) for j in range(1, modules // 2)]
    mine = ask(send, rotator, inverse, blocks)
    other, turned = turn(after(swap(bases, "module", 1), mine), rotator, pairs[0])
    turned = [turned, *turn_more(rotator, other, sent)]
    theirs = [swap(mine, "group", near) for near in range(1, inner)]
    others = [(own, swap(after(own, *turned), "module", 1)) for own in theirs]
    factor = 1.0 / math.sqrt(modules * width)
    parts = score(pick, (mine, swap(mine, "module", 1)), others, turned, factor)
    total = parts[0]
    for j in range(1, modules // 2):
        total = total + swap(parts[j], "module", 2 * j)
    return total


def solution(mesh):
    in_specs = (
        P(("group", "module"), None, None),
        P("group", None, "module", None),
        P("module", None, None),
        P("module", None, None),
        P("module", None),
        P(),
        P(),
    )
    out_specs = P(("group", "module"), None)
    return jax.shard_map(local, mesh=mesh, in_specs=in_specs, out_specs=out_specs, check_vma=False)
```

```python
import functools
import math

import jax
import jax.numpy as jnp
from jax import lax
from jax.experimental import pallas as pl
from jax.experimental.pallas import tpu as pltpu
from jax.sharding import PartitionSpec as P

LANES = 128
VMEM = pl.BlockSpec(memory_space=pltpu.VMEM)
HBM = pl.BlockSpec(memory_space=pltpu.HBM)
PARAMS = pltpu.CompilerParams(vmem_limit_bytes=32 * 1024 * 1024)


def place_of(owners, k, me, inner):
    seen = [owners[j] ^ me for j in range(owners.shape[0])]
    near, far = seen[k] % inner, seen[k] // inner
    place = jnp.int32(0)
    for other in seen:
        place += jnp.logical_and(other % inner == near, other // inner < far).astype(jnp.int32)
    return near, far, place


def build_rotator(basis_out, basis_in, rotator_ref):
    side, width = basis_out.shape[0], rotator_ref.shape[0]
    column = lax.broadcasted_iota(jnp.int32, (side, width), 1)
    row = lax.broadcasted_iota(jnp.int32, (side, width), 0)
    spread = (column // side == row).astype(jnp.bfloat16)
    tiled = (column % side == row).astype(jnp.bfloat16)
    outer = jnp.dot(basis_out, spread, preferred_element_type=jnp.float32)
    inside = jnp.dot(basis_in, tiled, preferred_element_type=jnp.float32)
    for a in range(side):
        rotator_ref[pl.ds(a * side, side), :] = (outer[a : a + 1, :] * inside).astype(jnp.bfloat16)


def prepare_kernel(inner, each, order_hbm, owners_hbm, out_hbm, in_hbm, values_hbm, own_hbm, train_hbm, *refs):
    rotator_ref, inverse_ref, send_ref, pick_ref, own_ref, bases_ref, *pairs = refs[:-8]
    order, owners, out_ref, in_ref, values, train, wide, sems = refs[-8:]
    loads = [
        pltpu.make_async_copy(src, dst, sems.at[i])
        for i, (src, dst) in enumerate(
            (
                (out_hbm, out_ref),
                (in_hbm, in_ref),
                (order_hbm, order),
                (owners_hbm, owners),
                (values_hbm, values),
                (own_hbm, own_ref),
                (train_hbm, train),
            )
        )
    ]
    for load in loads:
        load.start()
    side, width = out_ref.shape[1], rotator_ref.shape[0]
    for load in loads[:2]:
        load.wait()
    bases_ref[:side, :] = out_ref[0]
    bases_ref[side:, :] = in_ref[0]
    build_rotator(out_ref[0], in_ref[0], rotator_ref)
    for load in loads[2:]:
        load.wait()
    spectrum = values[...]
    inverse_ref[...] = 1.0 / (spectrum + 0.1 * jnp.mean(spectrum, axis=1, keepdims=True))

    me = lax.axis_index("group")
    places = send_ref.shape[0] // each
    line = lax.broadcasted_iota(jnp.int32, send_ref.shape, 0)
    lane = lax.broadcasted_iota(jnp.int32, send_ref.shape, 1)
    send = jnp.zeros(send_ref.shape, jnp.float32)
    line_p = lax.broadcasted_iota(jnp.int32, pick_ref.shape, 0)
    lane_p = lax.broadcasted_iota(jnp.int32, pick_ref.shape, 1)
    pick = jnp.zeros(pick_ref.shape, jnp.float32)
    for k in range(owners.shape[0]):
        near, far, place = place_of(owners, k, me, inner)
        shift = jnp.where(near == 0, (far - place) * each, -2 * send_ref.shape[1])
        hit = jnp.logical_and(lane - line == shift, line // each == place)
        send = jnp.where(hit, 1.0, send)
        shift = (near * places + place - k) * each
        hit = jnp.logical_and(lane_p - line_p == shift, line_p // each == k)
        pick = jnp.where(hit, 1.0, pick)
    send_ref[...] = send.astype(jnp.bfloat16)
    pick_ref[...] = pick.astype(jnp.bfloat16)

    rows, modules, _ = train.shape
    tiles = width // LANES
    slot = lax.axis_index("module")
    for e in range(rows):
        example = train[e].astype(jnp.float32)
        for t in range(tiles):
            wide[pl.ds((t * rows + e) * modules, modules), :] = example[:, t * LANES : (t + 1) * LANES]
    for j in range(modules):
        held = order[slot ^ j]
        out, at = (pairs[0], j * rows) if j < 2 else (pairs[j - 1], 0)
        for t in range(tiles):
            piece = wide[pl.ds(t * rows * modules + held, rows, stride=modules), :]
            out[at : at + rows, t * LANES : (t + 1) * LANES] = piece.astype(out.dtype)


def prepare(train_grads, own, basis_out, basis_in, eigenvalues, owner_groups, module_order, inner, blocks):
    each = own.shape[0]
    rows, modules, width = train_grads.shape
    asked = owner_groups.shape[0]
    places = min(blocks, asked - (inner > 1))
    pair = jax.ShapeDtypeStruct((2 * rows, width), train_grads.dtype)
    shapes = (
        jax.ShapeDtypeStruct((width, width), jnp.bfloat16),
        jax.ShapeDtypeStruct(eigenvalues.shape, jnp.float32),
        jax.ShapeDtypeStruct((places * each, blocks * each), jnp.bfloat16),
        jax.ShapeDtypeStruct((asked * each, inner * places * each), jnp.bfloat16),
        jax.ShapeDtypeStruct(own.shape, own.dtype),
        jax.ShapeDtypeStruct((2 * basis_out.shape[1], basis_out.shape[2]), basis_out.dtype),
    ) + (pair,) + (jax.ShapeDtypeStruct((rows, width), train_grads.dtype),) * (modules - 2)
    return pl.pallas_call(
        functools.partial(prepare_kernel, inner, each),
        out_shape=shapes,
        in_specs=[HBM] * 7,
        out_specs=(VMEM,) * len(shapes),
        scratch_shapes=[
            pltpu.SMEM(module_order.shape, jnp.int32),
            pltpu.SMEM(owner_groups.shape, jnp.int32),
            pltpu.VMEM(basis_out.shape, basis_out.dtype),
            pltpu.VMEM(basis_in.shape, basis_in.dtype),
            pltpu.VMEM(eigenvalues.shape, eigenvalues.dtype),
            pltpu.VMEM(train_grads.shape, train_grads.dtype),
            pltpu.VMEM((rows * modules * width // LANES + modules, LANES), jnp.float32),
            pltpu.SemaphoreType.DMA((7,)),
        ],
        compiler_params=PARAMS,
    )(
        *(
            pltpu.with_memory_space_constraint(operand, pltpu.HBM)
            for operand in (module_order, owner_groups, basis_out, basis_in, eigenvalues, own, train_grads)
        )
    )


def ask_kernel(order, send_ref, rotator_ref, inverse_ref, *refs):
    *blocks, out = refs
    queries = jnp.dot(
        send_ref[...],
        jnp.concatenate([blocks[order.index(b)][...] for b in range(len(order))], axis=0),
        preferred_element_type=jnp.float32,
    )
    out[...] = (
        inverse_ref[...]
        * jnp.dot(queries.astype(jnp.bfloat16), rotator_ref[...], preferred_element_type=jnp.float32)
    ).astype(out.dtype)


def ask(send, rotator, inverse, blocks):
    order = (*range(2, len(blocks)), 1, 0)
    return pl.pallas_call(
        functools.partial(ask_kernel, order),
        out_shape=jax.ShapeDtypeStruct((send.shape[0], rotator.shape[0]), jnp.bfloat16),
        in_specs=[VMEM] * (3 + len(blocks)),
        out_specs=VMEM,
        compiler_params=PARAMS,
    )(send, rotator, inverse, *(blocks[b] for b in order))


def turn_kernel(bases_ref, rotator_ref, pair, other_ref, *outs):
    rows, side = pair.shape[0] // 2, bases_ref.shape[1]
    build_rotator(bases_ref[:side, :], bases_ref[side:, :], other_ref)
    for half, (rotator, out) in enumerate(zip((rotator_ref, other_ref), outs)):
        out[...] = jnp.dot(
            pair[half * rows : (half + 1) * rows, :], rotator[...], preferred_element_type=jnp.float32
        ).astype(out.dtype)


def turn(bases, rotator, pair):
    half = jax.ShapeDtypeStruct((pair.shape[0] // 2, pair.shape[1]), pair.dtype)
    return pl.pallas_call(
        turn_kernel,
        out_shape=(jax.ShapeDtypeStruct(rotator.shape, rotator.dtype), half, half),
        in_specs=[VMEM] * 3,
        out_specs=(VMEM,) * 3,
        compiler_params=PARAMS,
    )(bases, rotator, pair)


def turn_more_kernel(rotator_ref, other_ref, *refs):
    pieces, outs = refs[:-2], refs[-2:]
    for half, (rotator, out) in enumerate(zip((rotator_ref, other_ref), outs)):
        out[...] = jnp.dot(
            jnp.concatenate([piece[...] for piece in pieces[half::2]], axis=0),
            rotator[...],
            preferred_element_type=jnp.float32,
        ).astype(out.dtype)


def turn_more(rotator, other, pieces):
    rows, width = pieces[0].shape
    shape = jax.ShapeDtypeStruct((rows * (len(pieces) // 2), width), pieces[0].dtype)
    return pl.pallas_call(
        turn_more_kernel,
        out_shape=(shape,) * 2,
        in_specs=[VMEM] * (2 + len(pieces)),
        out_specs=(VMEM,) * 2,
        compiler_params=PARAMS,
    )(rotator, other, *pieces)


def scores_of(turned, pick_ref, first, columns):
    span = columns[0].shape[0]
    asked = jnp.dot(
        pick_ref[:, first * span : (first + len(columns)) * span],
        jnp.concatenate([places[...] for places in columns], axis=0),
        preferred_element_type=jnp.float32,
    ).astype(jnp.bfloat16)
    return lax.dot_general(
        jnp.concatenate([part[...] for part in turned], axis=0),
        asked,
        (((1,), (1,)), ((), ())),
        preferred_element_type=jnp.float32,
    )


def score_kernel(factor, pick_ref, mine_ref, *refs):
    (near, far, near_got, far_got), refs = refs[:4], refs[4:]
    rows = near.shape[0]
    count = 2 + 2 * (far.shape[0] // rows)
    theirs, outs = refs[:-count], refs[-count:]
    total = scores_of([near, far, near_got, far_got], pick_ref, 0, [mine_ref, *theirs])
    for j, out in enumerate(outs):
        at = (j % 2 * (count // 2) + j // 2) * rows
        out[...] = factor * total[at : at + rows, :]


def score(pick, mine, turned, theirs, factor):
    rows = turned[0].shape[0]
    count = 2 + 2 * (turned[1].shape[0] // rows)
    return pl.pallas_call(
        functools.partial(score_kernel, factor),
        out_shape=(jax.ShapeDtypeStruct((rows, pick.shape[0]), jnp.float32),) * count,
        in_specs=[VMEM] * (2 + len(turned) + len(theirs)),
        out_specs=(VMEM,) * count,
        compiler_params=PARAMS,
    )(pick, mine, *turned, *theirs)


def swap(array, axis, bits):
    return lax.ppermute(array, axis, [(i, i ^ bits) for i in range(lax.axis_size(axis))])


def after(array, *others):
    return lax.optimization_barrier((array,) + others)[0]


def local(train_grads, query_grads, basis_out, basis_in, eigenvalues, owner_groups, module_order):
    _, modules, width = train_grads.shape
    groups = lax.axis_size("group")
    inner = 1 << ((groups.bit_length() - 1) // 2)
    own = query_grads.reshape(-1, width)
    each = own.shape[0]
    blocks = [own] + [swap(own, "group", far) for far in range(inner, groups, inner)]
    rotator, inverse, send, pick, own, bases, *pairs = prepare(
        train_grads,
        own,
        basis_out,
        basis_in,
        eigenvalues,
        owner_groups,
        module_order,
        inner,
        len(blocks),
    )
    blocks[0] = own
    sent = [swap(pairs[j - 1], "module", j - j % 2) for j in range(2, modules)]
    mine = ask(send, rotator, inverse, blocks)
    other, near, near_other = turn(after(swap(bases, "module", 1), mine), rotator, pairs[0])
    far, far_other = turn_more(rotator, other, sent)
    theirs = [swap(mine, "group", column) for column in range(1, inner)]
    factor = 1.0 / math.sqrt(modules * width)
    got = [swap(near_other, "module", 1), swap(far_other, "module", 1)]
    parts = score(pick, mine, (near, far, *got), theirs, factor)
    total = parts[0]
    for j in range(1, modules):
        total = total + swap(parts[j], "module", j)
    return total


def solution(mesh):
    in_specs = (
        P(("group", "module"), None, None),
        P("group", None, "module", None),
        P("module", None, None),
        P("module", None, None),
        P("module", None),
        P(),
        P(),
    )
    out_specs = P(("group", "module"), None)
    return jax.shard_map(local, mesh=mesh, in_specs=in_specs, out_specs=out_specs, check_vma=False)
```
